256 devices in a mesh: row: 32 (over z, x), col: 8 (over y, core).
Axes of the slice: x: 4, y: 4, z: 8, core: 2. Of those that a mesh axis runs over, the one named last changes fastest.
Arguments:
- tile_values: bfloat16 [16384, 128, 128], P(('row', 'col')), may hold values from 0 to 327680
- tile_places: int32 [16384, 2], P(('row', 'col')), may hold values from 0 to 63, as said below
- tile_counts: int32 [256], P(('row', 'col')), may hold values from 8 to 64, as said below
- doc_factor: bfloat16 [131072, 256], P(('row', 'col')), may hold values from 0 to 2
- term_factor: bfloat16 [65536, 256], P(('col', 'row')), may hold values from 0 to 5
Outputs:
- new_doc_factor: bfloat16 [131072, 256], P(('row', 'col'))
- new_term_factor: bfloat16 [65536, 256], P(('col', 'row'))
The draws below stay inside these ranges and needn't reach their ends.
Inputs may be any that keep to these rules, and one draw needn't show every extreme that they name: `tile_places`: each entry is a tile row below 32 and a tile column below 64; the 64 positions of one device are all different. `tile_counts`: some device uses all 64 slots.
All inputs are finite; a program needn't handle non-finite values.
Results may differ from the reference program's by a relative error of at most 0.01425.
Values may be sent and summed in bfloat16 or wider, within the bound.
No kernel may reach another device: no remote copies, remote signals or barrier semaphores. Data moves between devices by JAX's collectives and lax.ppermute only.
A program may use at most 128 MiB of HBM per device.

```python
import math
import jax
import jax.numpy as jnp
from jax import lax

RANK = 256
TILE = 128
CAP = 64
SWEEPS = 1
TILE_ROWS = 32
TILE_COLS = 64
DOCS = 131072
TERMS = 65536
N_ROW = 32
N_COL = 8


def draw_tile_values(key, part):
    key = jax.random.fold_in(key, 11)
    keys = jax.random.split(key, 3)
    slots = N_ROW * N_COL * CAP
    row_scale = jnp.exp(jax.random.uniform(keys[0], (slots, TILE, 1), dtype=jnp.float32, minval=-1.2, maxval=1.2))
    col_scale = jnp.exp(jax.random.uniform(keys[1], (slots, 1, TILE), dtype=jnp.float32, minval=-1.2, maxval=1.2))
    noise = jax.random.uniform(keys[2], (slots, TILE, TILE), dtype=jnp.float32)
    noise = 2.0 * noise
    amplitude = RANK * TILE_ROWS * TILE_COLS / (0.56 * CAP)
    return (amplitude * row_scale * col_scale * noise).astype(jnp.bfloat16)


def draw_tile_places(key, part):
    key = jax.random.fold_in(key, 23)
    devices = N_ROW * N_COL
    slots = TILE_ROWS * TILE_COLS
    scores = jax.random.randint(key, (devices, slots), 0, 4096, dtype=jnp.int32) * slots + jnp.arange(slots, dtype=jnp.int32)[None, :]
    order = jnp.argsort(scores, axis=1)[:, :CAP].astype(jnp.int32)
    places = jnp.stack([order // TILE_COLS, order % TILE_COLS], axis=-1)
    return places.reshape(devices * CAP, 2).astype(jnp.int32)


def draw_tile_counts(key, part):
    key = jax.random.fold_in(key, 37)
    keys = jax.random.split(key, 2)
    devices = N_ROW * N_COL
    spread = jax.random.randint(keys[0], (devices,), 0, CAP + 1, dtype=jnp.int32)
    counts = jnp.maximum(CAP // 8, spread * spread // CAP)
    busiest = jax.random.randint(keys[1], (), 0, devices, dtype=jnp.int32)
    return jnp.where(jnp.arange(devices, dtype=jnp.int32) == busiest, CAP, counts).astype(jnp.int32)


def draw_term_factor(key, part):
    key = jax.random.fold_in(key, 7)
    keys = jax.random.split(key, 1)
    position = jnp.arange(TERMS, dtype=jnp.float32)[:, None] / TERMS
    noise = jax.random.uniform(keys[0], (TERMS, RANK), dtype=jnp.float32)
    return (noise * (1.0 + 2.0 * position)).astype(jnp.bfloat16)


def levels(rng, dims, cuts, smallest, largest):
    gain, own = 1.0, jax.random.fold_in(rng, 6)
    for axis_at, parts in cuts:
        steps = jnp.exp(jax.random.uniform(jax.random.fold_in(own, axis_at), (parts,), jnp.float32, smallest / len(cuts), largest / len(cuts)))
        gain = gain * jnp.repeat(steps, dims[axis_at] // parts).reshape([-1 if axis == axis_at else 1 for axis in range(len(dims))])
    return gain


def setup_inputs(seed: int = 0) -> dict:
    arg_keys = jax.random.split(jax.random.key(seed), 6)
    return {
        "tile_values": draw_tile_values(jax.random.fold_in(arg_keys[5], 71), 0),
        "tile_places": draw_tile_places(jax.random.fold_in(arg_keys[5], 71), 0),
        "tile_counts": draw_tile_counts(jax.random.fold_in(arg_keys[5], 71), 0),
        "doc_factor": jnp.clip(2.0 * jax.random.uniform(arg_keys[3], (DOCS, RANK), jnp.float32) ** levels(arg_keys[3], (DOCS, RANK), ((0, 256),), -0.2, 0.2), 0.0, 2.0).astype(jnp.bfloat16),
        "term_factor": draw_term_factor(jax.random.fold_in(arg_keys[5], 71), 0),
    }


sweep_width = 16


def gram_of(factor_rows):
    return lax.dot_general(factor_rows, factor_rows, (((0,), (0,)), ((), ())), preferred_element_type=jnp.float32)


def forward_block(block_tiles, block_places, live_count, panel_rows, tile_rows):
    tile_size = block_tiles.shape[1]
    rank_width = panel_rows.shape[1]
    panel_tiles = panel_rows.reshape(-1, tile_size, rank_width)
    group_size = math.gcd(block_tiles.shape[0], 32)

    def add_group(group_index, running):
        offset = group_index * group_size
        tiles_now = lax.dynamic_slice_in_dim(block_tiles, offset, group_size, 0).astype(jnp.float32)
        places_now = lax.dynamic_slice_in_dim(block_places, offset, group_size, 0)
        active = (offset + jnp.arange(group_size, dtype=jnp.int32) < live_count).astype(jnp.float32)
        chosen = jnp.take(panel_tiles, places_now[:, 1], axis=0).astype(jnp.float32)
        product = jnp.einsum("gab,gbk->gak", tiles_now, chosen, precision=lax.Precision.HIGHEST)
        return running.at[places_now[:, 0]].add(product * active[:, None, None])

    running = jnp.zeros((tile_rows, tile_size, rank_width), jnp.float32)
    running = lax.fori_loop(0, block_tiles.shape[0] // group_size, add_group, running)
    return running.reshape(tile_rows * tile_size, rank_width)


def backward_block(block_tiles, block_places, live_count, panel_rows, tile_cols):
    tile_size = block_tiles.shape[1]
    rank_width = panel_rows.shape[1]
    panel_tiles = panel_rows.reshape(-1, tile_size, rank_width)
    group_size = math.gcd(block_tiles.shape[0], 32)

    def add_group(group_index, running):
        offset = group_index * group_size
        tiles_now = lax.dynamic_slice_in_dim(block_tiles, offset, group_size, 0).astype(jnp.float32)
        places_now = lax.dynamic_slice_in_dim(block_places, offset, group_size, 0)
        active = (offset + jnp.arange(group_size, dtype=jnp.int32) < live_count).astype(jnp.float32)
        chosen = jnp.take(panel_tiles, places_now[:, 0], axis=0).astype(jnp.float32)
        product = jnp.einsum("gab,gak->gbk", tiles_now, chosen, precision=lax.Precision.HIGHEST)
        return running.at[places_now[:, 1]].add(product * active[:, None, None])

    running = jnp.zeros((tile_cols, tile_size, rank_width), jnp.float32)
    running = lax.fori_loop(0, block_tiles.shape[0] // group_size, add_group, running)
    return running.reshape(tile_cols * tile_size, rank_width)


def hals_update(start_values, target, gram_matrix):
    rank_width = gram_matrix.shape[0]

    def one_block(block_index, current):
        offset = block_index * sweep_width
        gram_cols = lax.dynamic_slice_in_dim(gram_matrix, offset, sweep_width, 1)
        gram_square = lax.dynamic_slice_in_dim(gram_cols, offset, sweep_width, 0)
        remain = lax.dynamic_slice_in_dim(target, offset, sweep_width, 1) - jnp.dot(current, gram_cols, precision=lax.Precision.HIGHEST, preferred_element_type=jnp.float32)
        columns = lax.dynamic_slice_in_dim(current, offset, sweep_width, 1)
        updated = []
        for column in range(sweep_width):
            pivot = gram_square[column, column] + 1e-6
            fresh = jnp.maximum(columns[:, column] + remain[:, column] / pivot, 0.0)
            remain = remain - (fresh - columns[:, column])[:, None] * gram_square[column][None, :]
            updated.append(fresh)
        return lax.dynamic_update_slice_in_dim(current, jnp.stack(updated, axis=1), offset, 1)

    current = start_values
    for sweep_index in range(SWEEPS):
        current = lax.fori_loop(0, rank_width // sweep_width, one_block, current)
    return current


def reference(tile_values, tile_places, tile_counts, doc_factor, term_factor):
    tiles_grid = tile_values.reshape(N_ROW, N_COL, CAP, TILE, TILE)
    places_grid = tile_places.reshape(N_ROW, N_COL, CAP, 2)
    counts_grid = tile_counts.reshape(N_ROW, N_COL)
    term_blocks = term_factor.reshape(N_COL, TILE_COLS * TILE, RANK)
    column_ids = jnp.arange(N_COL, dtype=jnp.int32)
    row_ids = jnp.arange(N_ROW, dtype=jnp.int32)

    def doc_block(row_index):
        def add_column(running, column_index):
            term_part = forward_block(tiles_grid[row_index, column_index], places_grid[row_index, column_index], counts_grid[row_index, column_index], term_blocks[column_index], TILE_ROWS)
            return running + term_part, None
        start_sum = jnp.zeros((TILE_ROWS * TILE, RANK), jnp.float32)
        return lax.scan(add_column, start_sum, column_ids)[0]

    doc_target = lax.map(doc_block, row_ids).reshape(DOCS, RANK)
    term_gram = gram_of(term_factor)
    new_doc = hals_update(doc_factor.astype(jnp.float32), doc_target, term_gram).astype(jnp.bfloat16)
    doc_blocks = new_doc.reshape(N_ROW, TILE_ROWS * TILE, RANK)

    def term_block(column_index):
        def add_row(running, row_index):
            term_part = backward_block(tiles_grid[row_index, column_index], places_grid[row_index, column_index], counts_grid[row_index, column_index], doc_blocks[row_index], TILE_COLS)
            return running + term_part, None
        start_sum = jnp.zeros((TILE_COLS * TILE, RANK), jnp.float32)
        return lax.scan(add_row, start_sum, row_ids)[0]

    term_target = lax.map(term_block, column_ids).reshape(TERMS, RANK)
    doc_gram = gram_of(new_doc)
    new_term = hals_update(term_factor.astype(jnp.float32), term_target, doc_gram).astype(jnp.bfloat16)
    return new_doc, new_term
```

```python
import functools

import jax
import jax.numpy as jnp
from jax import lax
from jax.experimental import pallas as pl
from jax.experimental.pallas import tpu as pltpu
from jax.sharding import PartitionSpec as P

bf16, f16, f32 = jnp.bfloat16, jnp.float16, jnp.float32
NX, NZ, NY = 4, 8, 4
TILE, RANK = 128, 256
GROUP = 4
BLOCK = 64
EPS = 1e-06
NOTE = 16
VMEM_BYTES = 48 << 20

IN_VMEM = pl.BlockSpec(memory_space=pltpu.VMEM)
IN_SMEM = pl.BlockSpec(memory_space=pltpu.SMEM)
ANYWHERE = pl.BlockSpec(memory_space=pl.ANY)
CONTRACT_0 = (((0,), (0,)), ((), ()))
CONTRACT_1 = (((1,), (1,)), ((), ()))


def from_x(a, d):
    pairs = [(z * NX + (x + d) % NX, z * NX + x) for z in range(NZ) for x in range(NX)]
    return lax.ppermute(a, "row", pairs)


def from_z(a, d):
    pairs = [((z + d) % NZ * NX + x, z * NX + x) for z in range(NZ) for x in range(NX)]
    return lax.ppermute(a, "row", pairs)


def from_y(a, d):
    pairs = [((y + d) % NY * 2 + c, y * 2 + c) for y in range(NY) for c in range(2)]
    return lax.ppermute(a, "col", pairs)


def from_core(a):
    return lax.ppermute(a, "col", [(y * 2 + 1 - c, y * 2 + c) for y in range(NY) for c in range(2)])


def swap_x(a, hop):
    return lax.ppermute(a, "row", [(r ^ hop, r) for r in range(NZ * NX)])


def swap_z(a, hop):
    return lax.ppermute(a, "row", [(r ^ (hop * NX), r) for r in range(NZ * NX)])


def swap_y(a, hop):
    return lax.ppermute(a, "col", [(c ^ (hop * 2), c) for c in range(2 * NY)])


def add(first, *rest):
    total = first.astype(f32)
    for term in rest:
        total = total + term.astype(f32)
    return total


def gather_direct(a, n, step):
    return [a] + [step(a, d) for d in range(1, n)]


def gather_ring(a, n, step, way):
    out = [None] * n
    out[0] = up = down = a
    for d in range(1, n // 2):
        up, down = step(up, 1), step(down, -1)
        out[d], out[n - d] = up, down
    out[n // 2] = step(up, 1) if way > 0 else step(down, -1)
    return out


def exponent_rows(e):
    return jnp.broadcast_to(e, (NOTE, RANK))


def note_of(v):
    return v[-NOTE : 1 - NOTE].astype(f32)


def encode(v, e):
    row = lax.broadcasted_iota(jnp.int32, v.shape, 0)
    return jnp.where(row < v.shape[0] - NOTE, v * jnp.exp2(-e), e).astype(f16)


def encode_rows(v, e):
    return jnp.concatenate([v * jnp.exp2(-e), exponent_rows(e)], 0).astype(f16)


def decode_all(m):
    return m.astype(f32) * jnp.exp2(note_of(m))


def decode(m):
    return decode_all(m)[:-NOTE]


def double(a, step, n):
    hop = 1
    while hop < n:
        a = a + step(a, hop)
        hop *= 2
    return a


def start_copies(pairs, sems):
    copies = [pltpu.make_async_copy(src, dst, sems.at[i]) for i, (src, dst) in enumerate(pairs)]
    for copy in copies:
        copy.start()
    return copies


def rows_at(ref, index, size):
    return ref.at[pl.ds(pl.multiple_of(index * size, size), size)]


def gram_into(ref, panel):
    rows = panel.shape[0]
    total = jnp.zeros((RANK, RANK), f32)
    for at in range(0, rows, 1024):
        part = panel[at : at + 1024, :]
        total = total + lax.dot_general(part, part, CONTRACT_0, preferred_element_type=f32)
    ref[...] = total


def write_noted(out, acc, first, count):
    tiles = acc[first : first + count]
    rows = count * TILE
    out[0:rows, :] = tiles.reshape(rows, RANK)
    top = jnp.max(jnp.max(tiles.reshape(rows // 8, 8, RANK), axis=0), axis=0, keepdims=True)
    e = jnp.ceil(jnp.log(jnp.maximum(top, 1e-30)) * 1.4426950408889634) - 15.0
    out[rows:, :] = jnp.broadcast_to(e, (NOTE, RANK))


def tile_sums(count, places, tiles, panel, acc, slot_index, panel_side, dims):
    n = count[0]
    spare = acc.shape[0] - 1

    def group(i, carry):
        targets, products = [], []
        for q in range(GROUP):
            s = i * GROUP + q
            p0, p1 = places[s, 0], places[s, 1]
            targets.append(jnp.where(s < n, slot_index(p0, p1), spare))
            at = pl.multiple_of((p0, p1)[panel_side] * TILE, TILE)
            products.append(
                lax.dot_general(tiles[s], panel[pl.ds(at, TILE), :], dims, preferred_element_type=f32)
            )
        for target, product in zip(targets, products):
            acc[target] += product
        return carry

    lax.fori_loop(0, (n + GROUP - 1) // GROUP, group, 0)


def forward_kernel(where, ids, places, count, tiles, *refs):
    chunks = refs[: len(where)]
    own, other, gram_own, gram_other, acc, panel, tiles_here, gram, sems = refs[len(where) :]
    z, x, y, core = ids[0], ids[1], ids[2], ids[3]
    pairs = [(tiles, tiles_here)]
    for chunk, places_of in zip(chunks, where):
        for k, (dz, dx, h) in enumerate(places_of):
            row = ((z + dz) & (NZ - 1)) * NX + ((x + dx) & (NX - 1))
            pairs.append((chunk.at[pl.ds(k * TILE, TILE)], rows_at(panel, row * 2 + h, TILE)))
    copies = start_copies(pairs, sems)
    acc[...] = jnp.zeros_like(acc)
    for copy in copies:
        copy.wait()

    def slot_index(p0, p1):
        c = p0 // 4
        return ((c & 1) ^ core) * 16 + ((c // 2 - y) & (NY - 1)) * 4 + (p0 & 3)

    tile_sums(count, places, tiles_here, panel, acc, slot_index, 1, (((1,), (0,)), ((), ())))
    for d in range(NY):
        write_noted(own.at[d], acc, 4 * d, 4)
        write_noted(other.at[d], acc, 16 + 4 * d, 4)
    gram_into(gram, panel)
    half = RANK // 2
    gram_own[...] = gram[pl.ds(pl.multiple_of(core * half, half), half), :]
    gram_other[...] = gram[pl.ds(pl.multiple_of((1 - core) * half, half), half), :]


def forward(ids, places, count, tiles, where, chunks):
    slots = tiles.shape[0]
    n_copies = 1 + sum(len(w) for w in where)
    return pl.pallas_call(
        functools.partial(forward_kernel, where),
        out_shape=[
            jax.ShapeDtypeStruct((NY, 512 + NOTE, RANK), f32),
            jax.ShapeDtypeStruct((NY, 512 + NOTE, RANK), f32),
            jax.ShapeDtypeStruct((RANK // 2, RANK), f32),
            jax.ShapeDtypeStruct((RANK // 2, RANK), f32),
        ],
        in_specs=[IN_SMEM] * 3 + [ANYWHERE] * (1 + len(chunks)),
        out_specs=[IN_VMEM] * 4,
        scratch_shapes=[
            pltpu.VMEM((33, TILE, RANK), f32),
            pltpu.VMEM((8192, RANK), bf16),
            pltpu.VMEM((slots, TILE, TILE), bf16),
            pltpu.VMEM((RANK, RANK), f32),
            pltpu.SemaphoreType.DMA((n_copies,)),
        ],
        compiler_params=pltpu.CompilerParams(vmem_limit_bytes=VMEM_BYTES),
        name="forward",
    )(ids, places, count, tiles, *chunks)


def backward_kernel(ids, places, count, tiles, *refs):
    near, far = refs[:NY], refs[NY : 2 * NY]
    out_x, out_z, gram_rows, acc, panel, tiles_here, gram, sems = refs[2 * NY :]
    z, x, y, core = ids[0], ids[1], ids[2], ids[3]
    pairs = [(tiles, tiles_here)]
    for d in range(NY):
        at = ((y + d) & (NY - 1)) * 2
        pairs.append((near[d], rows_at(panel, at + core, 512)))
        pairs.append((far[d], rows_at(panel, at + 1 - core, 512)))
    copies = start_copies(pairs, sems)
    acc[...] = jnp.zeros_like(acc)
    for copy in copies:
        copy.wait()

    def slot_index(p0, p1):
        r = p1 // 2
        dz = (r // NX - z) & (NZ - 1)
        dx = (r - x) & (NX - 1)
        return jnp.where((p1 & 1) == 0, dx * NZ + dz, NX * NZ + dz * NX + dx)

    tile_sums(count, places, tiles_here, panel, acc, slot_index, 0, CONTRACT_0)
    for d in range(NX):
        write_noted(out_x.at[d], acc, NZ * d, NZ)
    for d in range(NZ):
        write_noted(out_z.at[d], acc, NX * NZ + NX * d, NX)
    gram_into(gram, panel)
    gram_rows[...] = gram[pl.ds(pl.multiple_of((y * 2 + core) * 32, 32), 32), :]


def backward(ids, places, count, tiles, near, far):
    slots = tiles.shape[0]
    return pl.pallas_call(
        backward_kernel,
        out_shape=[
            jax.ShapeDtypeStruct((NX, NZ * TILE + NOTE, RANK), f32),
            jax.ShapeDtypeStruct((NZ, NX * TILE + NOTE, RANK), f32),
            jax.ShapeDtypeStruct((32, RANK), f32),
        ],
        in_specs=[IN_SMEM] * 3 + [ANYWHERE] * (1 + 2 * NY),
        out_specs=[IN_VMEM] * 3,
        scratch_shapes=[
            pltpu.VMEM((65, TILE, RANK), f32),
            pltpu.VMEM((4096, RANK), bf16),
            pltpu.VMEM((slots, TILE, TILE), bf16),
            pltpu.VMEM((RANK, RANK), f32),
            pltpu.SemaphoreType.DMA((1 + 2 * NY,)),
        ],
        compiler_params=pltpu.CompilerParams(vmem_limit_bytes=VMEM_BYTES),
        name="backward",
    )(ids, places, count, tiles, *near, *far)


def hals_kernel(groups, gram_pieces, ids, x_ref, near_ref, far_ref, *refs):
    n_parts = sum(count for _, count in groups)
    parts = refs[:n_parts]
    out_ref, xt, rt, gram = refs[n_parts:]
    n = x_ref.shape[0]
    y, core = ids[2], ids[3]
    size = RANK // (2 * gram_pieces)
    for d in range(gram_pieces):
        at = (y ^ d) * 2 if gram_pieces > 1 else 0
        for ref, c in ((near_ref, core), (far_ref, 1 - core)):
            gram[pl.ds(pl.multiple_of((at + c) * size, size), size), :] = ref[d * size : (d + 1) * size, :]
    g = gram[...]
    high = g.astype(bf16)
    rest = g - high.astype(f32)
    mid = rest.astype(bf16)
    low = (rest - mid.astype(f32)).astype(bf16)
    x = x_ref[...]
    xt[...] = x.astype(f32).T
    xg = lax.dot_general(low, x, CONTRACT_1, preferred_element_type=f32)
    xg = xg + lax.dot_general(mid, x, CONTRACT_1, preferred_element_type=f32)
    xg = xg + lax.dot_general(high, x, CONTRACT_1, preferred_element_type=f32)
    at = row = 0
    for rows, count in groups:
        target = add(*[part[...] for part in parts[at : at + count]])
        rt[:, row : row + rows] = target.T - xg[:, row : row + rows]
        at, row = at + count, row + rows
    shape = (RANK, RANK)
    diagonal = lax.broadcasted_iota(jnp.int32, shape, 0) == lax.broadcasted_iota(jnp.int32, shape, 1)
    inverse = 1.0 / (jnp.sum(jnp.where(diagonal, g, 0.0), axis=1, keepdims=True) + EPS)
    sublane = lax.broadcasted_iota(jnp.int32, (8, n), 0)
    for first in range(0, RANK, BLOCK):
        last = first + BLOCK
        remain = [rt[first + 8 * s : first + 8 * s + 8, :] for s in range(BLOCK // 8)]
        square = gram[first:last, first:last]
        changes = []
        for s in range(BLOCK // 8):
            at = first + 8 * s
            old = xt[at : at + 8, :]
            scale = jnp.broadcast_to(inverse[at : at + 8, :], (8, n))
            change = jnp.zeros((8, n), f32)
            for i in range(8):
                moved = jnp.maximum(old + remain[s] * scale, 0.0) - old
                change = jnp.where(sublane == i, moved, change)
                step = jnp.broadcast_to(moved[i : i + 1, :], (8, n))
                for t in range(s, BLOCK // 8):
                    remain[t] = remain[t] - square[8 * t : 8 * t + 8, 8 * s + i : 8 * s + i + 1] * step
            changes.append(change)
            xt[at : at + 8, :] = old + change
        if last < RANK:
            change = jnp.concatenate(changes, 0)
            change_high = change.astype(bf16)
            change_low = (change - change_high.astype(f32)).astype(bf16)
            update = jnp.dot(mid[last:, first:last], change_high, preferred_element_type=f32)
            update = update + jnp.dot(high[last:, first:last], change_low, preferred_element_type=f32)
            update = update + jnp.dot(high[last:, first:last], change_high, preferred_element_type=f32)
            rt[last:, :] = rt[last:, :] - update
    out_ref[...] = xt[...].T.astype(bf16)


def hals(ids, x, near, far, gram_pieces, groups):
    parts = [part for _, terms in groups for part in terms]
    spec = [(rows, len(terms)) for rows, terms in groups]
    n = x.shape[0]
    return pl.pallas_call(
        functools.partial(hals_kernel, spec, gram_pieces),
        out_shape=jax.ShapeDtypeStruct((n, RANK), bf16),
        in_specs=[IN_SMEM] + [IN_VMEM] * (3 + len(parts)),
        out_specs=IN_VMEM,
        scratch_shapes=[
            pltpu.VMEM((RANK, n), f32),
            pltpu.VMEM((RANK, n), f32),
            pltpu.VMEM((RANK, RANK), f32),
        ],
        compiler_params=pltpu.CompilerParams(vmem_limit_bytes=VMEM_BYTES),
        name="hals",
    )(ids, x, near, far, *parts)


def gather_terms(term_factor):
    first, second = term_factor[:TILE], term_factor[TILE:]
    along_x = jnp.concatenate(gather_direct(first, NX, from_x), 0)
    along_z = jnp.concatenate(gather_ring(second, NZ, from_z, -1), 0)
    chunks, where = [], []
    for dz, chunk in enumerate(gather_ring(along_x, NZ, from_z, 1)):
        chunks.append(chunk)
        where.append([(dz, dx, 0) for dx in range(NX)])
    for dx, chunk in enumerate(gather_direct(along_z, NX, from_x)):
        chunks.append(chunk)
        where.append([(dz, dx, 1) for dz in range(NZ)])
    return chunks, where


def sum_x_then_z(out_x):
    total, e = out_x[0][:-NOTE], note_of(out_x[0])
    for d in range(1, NX):
        m = from_x(encode(out_x[d], note_of(out_x[d])), -d)
        total, e = total + decode(m), jnp.maximum(e, note_of(m))
    e = e + 2.0
    rows = [total[TILE * d : TILE * (d + 1)] for d in range(NZ)]

    def hop(m, d, way):
        top = jnp.maximum(e, note_of(m)) + 1.0
        return from_z(encode_rows(rows[d] + decode(m), top), way)

    up = from_z(encode_rows(rows[4], e), -1)
    down = from_z(encode_rows(rows[5], e), 1)
    up = hop(up, 3, -1)
    down = hop(down, 6, 1)
    up = hop(up, 2, -1)
    down = hop(down, 7, 1)
    up = hop(up, 1, -1)
    return rows[0] + decode(up) + decode(down)


def sum_z_then_x(out_z):
    def hop(m, d, way):
        top = jnp.maximum(note_of(out_z[d]), note_of(m)) + 1.0
        return from_z(encode(out_z[d] + decode_all(m), top), way)

    up = from_z(encode(out_z[3], note_of(out_z[3])), -1)
    down = from_z(encode(out_z[4], note_of(out_z[4])), 1)
    up = hop(up, 2, -1)
    down = hop(down, 5, 1)
    up = hop(up, 1, -1)
    down = hop(down, 6, 1)
    down = hop(down, 7, 1)
    total = out_z[0][:-NOTE] + decode(up) + decode(down)
    e = jnp.maximum(jnp.maximum(note_of(out_z[0]), note_of(up)), note_of(down)) + 2.0
    rows = [total[TILE * d : TILE * (d + 1)] for d in range(NX)]
    result = rows[0]
    for d in range(1, NX):
        result = result + decode(from_x(encode_rows(rows[d], e), -d))
    return result


def shards(tile_values, tile_places, tile_counts, doc_factor, term_factor):
    row, col = lax.axis_index("row"), lax.axis_index("col")
    ids = jnp.stack([row // NX, row % NX, col // 2, col % 2]).astype(jnp.int32)

    with jax.named_scope("gather_terms"):
        chunks, where = gather_terms(term_factor)
    own, other, gram_near, gram_far = forward(ids, tile_places, tile_counts, tile_values, where, chunks)

    with jax.named_scope("sum_doc_target"):
        arrived = from_core(other)
        target = (own[0] + arrived[0])[:-NOTE]
        for d in range(1, NY):
            e = jnp.maximum(note_of(own[d]), note_of(arrived[d])) + 1.0
            target = target + decode(from_y(encode(own[d] + arrived[d], e), -d))
    with jax.named_scope("sum_term_gram"):
        gram_near = double(gram_near + from_core(gram_far), swap_y, NY)
        gram_far = from_core(gram_near)

    new_doc = hals(ids, doc_factor, gram_near, gram_far, 1, [(512, [target])])

    with jax.named_scope("gather_docs"):
        near = gather_direct(new_doc, NY, from_y)
        far = [from_core(chunk) for chunk in near]
    out_x, out_z, gram_rows = backward(ids, tile_places, tile_counts, tile_values, near, far)

    with jax.named_scope("sum_doc_gram"):
        gram_rows = double(double(gram_rows, swap_x, NX), swap_z, NZ)
        gram_near = jnp.concatenate([gram_rows, swap_y(gram_rows, 1)], 0)
        gram_near = jnp.concatenate([gram_near, swap_y(gram_near, 2)], 0)
        gram_far = from_core(gram_near)
    with jax.named_scope("sum_term_target"):
        first = sum_x_then_z(out_x)
        second = sum_z_then_x(out_z)

    new_term = hals(ids, term_factor, gram_near, gram_far, NY, [(TILE, [first]), (TILE, [second])])
    return new_doc, new_term


def solution(mesh):
    in_specs = (
        P(("row", "col"), None, None),
        P(("row", "col"), None),
        P(("row", "col")),
        P(("row", "col"), None),
        P(("col", "row"), None),
    )
    out_specs = (P(("row", "col"), None), P(("col", "row"), None))
    return jax.shard_map(shards, mesh=mesh, in_specs=in_specs, out_specs=out_specs, check_vma=False)
```

```python
import functools

import jax
import jax.numpy as jnp
from jax import lax
from jax.experimental import pallas as pl
from jax.experimental.pallas import tpu as pltpu
from jax.sharding import PartitionSpec as P

bf16, f16, f32 = jnp.bfloat16, jnp.float16, jnp.float32
NX, NZ, NY = 4, 8, 4
TILE, RANK = 128, 256
GROUP = 4
BLOCK = 64
EPS = 1e-06
NOTE = 16
VMEM_BYTES = 48 << 20

IN_VMEM = pl.BlockSpec(memory_space=pltpu.VMEM)
IN_SMEM = pl.BlockSpec(memory_space=pltpu.SMEM)
ANYWHERE = pl.BlockSpec(memory_space=pl.ANY)
CONTRACT_0 = (((0,), (0,)), ((), ()))
CONTRACT_1 = (((1,), (1,)), ((), ()))


def from_x(a, d):
    pairs = [(z * NX + (x + d) % NX, z * NX + x) for z in range(NZ) for x in range(NX)]
    return lax.ppermute(a, "row", pairs)


def from_z(a, d):
    pairs = [((z + d) % NZ * NX + x, z * NX + x) for z in range(NZ) for x in range(NX)]
    return lax.ppermute(a, "row", pairs)


def from_y(a, d):
    pairs = [((y + d) % NY * 2 + c, y * 2 + c) for y in range(NY) for c in range(2)]
    return lax.ppermute(a, "col", pairs)


def from_core(a):
    return lax.ppermute(a, "col", [(y * 2 + 1 - c, y * 2 + c) for y in range(NY) for c in range(2)])


def swap_z(a, hop):
    return lax.ppermute(a, "row", [(r ^ (hop * NX), r) for r in range(NZ * NX)])


def swap_y(a, hop):
    return lax.ppermute(a, "col", [(c ^ (hop * 2), c) for c in range(2 * NY)])


def after(values, deps):
    return lax.optimization_barrier((values, deps))[0]


def add(first, *rest):
    total = first.astype(f32)
    for term in rest:
        total = total + term.astype(f32)
    return total


def gather_direct(a, n, step):
    return [a] + [step(a, d) for d in range(1, n)]


def gather_ring(a, n, step, way):
    out = [None] * n
    out[0] = up = down = a
    for d in range(1, n // 2):
        up, down = step(up, 1), step(down, -1)
        out[d], out[n - d] = up, down
    out[n // 2] = step(up, 1) if way > 0 else step(down, -1)
    return out


def note_of(v):
    note = v[-NOTE:].astype(f32)
    return note[:1], note[NOTE // 2 : NOTE // 2 + 1] * 0.5


def wider(*notes):
    big, small = notes[0]
    for s, t in notes[1:]:
        big, small = jnp.maximum(big, s), jnp.minimum(small, t)
    return big, small


def encode(v, note):
    s, t = note
    row = lax.broadcasted_iota(jnp.int32, v.shape, 0) - (v.shape[0] - NOTE)
    return jnp.where(row < 0, v * ((t * t) * (t * t)), jnp.where(row < NOTE // 2, s, t * 2.0)).astype(f16)


def encode_each(v, note):
    s, t = note
    lines = [jnp.broadcast_to(line, (v.shape[0], NOTE // 2, RANK)) for line in (s, t * 2.0)]
    return jnp.concatenate([v * ((t * t) * (t * t))] + lines, 1).astype(f16)


def decode_all(m):
    s, _ = note_of(m)
    return m.astype(f32) * ((s * s) * (s * s))


def decode(m):
    return decode_all(m)[:-NOTE]


def decode_sum(m):
    s = m[:, -NOTE : 1 - NOTE].astype(f32)
    return jnp.sum(m[:, :-NOTE].astype(f32) * ((s * s) * (s * s)), 0)


def exchange_z(a):
    groups = [[z * NX + x for z in range(NZ)] for x in range(NX)]
    return lax.all_to_all(a, "row", 0, 0, axis_index_groups=groups)


def double(a, step, n):
    hop = 1
    while hop < n:
        a = a + step(a, hop)
        hop *= 2
    return a


def start_copies(pairs, sems):
    copies = [pltpu.make_async_copy(src, dst, sems.at[i]) for i, (src, dst) in enumerate(pairs)]
    for copy in copies:
        copy.start()
    return copies


def rows_at(ref, index, size):
    return ref.at[pl.ds(pl.multiple_of(index * size, size), size)]


def gram_into(ref, panel):
    rows = panel.shape[0]
    total = jnp.zeros((RANK, RANK), f32)
    for at in range(0, rows, 1024):
        part = panel[at : at + 1024, :]
        total = total + lax.dot_general(part, part, CONTRACT_0, preferred_element_type=f32)
    ref[...] = total


def write_noted(out, acc, first, count):
    tiles = acc[first : first + count]
    rows = count * TILE
    out[0:rows, :] = tiles.reshape(rows, RANK)
    top = jnp.max(jnp.max(tiles.reshape(rows // 8, 8, RANK), axis=0), axis=0, keepdims=True)
    e = jnp.ceil(jnp.log(jnp.maximum(top, 1e-30)) * 1.4426950408889634) - 11.0
    k = jnp.clip(jnp.ceil(e * 0.25), -14.0, 15.0)
    out[rows : rows + 8, :] = jnp.broadcast_to(jnp.exp2(k), (8, RANK))
    out[rows + 8 : rows + 16, :] = jnp.broadcast_to(jnp.exp2(1.0 - k), (8, RANK))


def tile_sums(count, places, tiles, panel, acc, slot_index, panel_tile, dims):
    n = count[0]
    spare = acc.shape[0] - 1

    def group(i, carry):
        targets, products = [], []
        for q in range(GROUP):
            s = i * GROUP + q
            p0, p1 = places[s, 0], places[s, 1]
            targets.append(jnp.where(s < n, slot_index(p0, p1), spare))
            at = pl.multiple_of(panel_tile(p0, p1) * TILE, TILE)
            products.append(
                lax.dot_general(tiles[s], panel[pl.ds(at, TILE), :], dims, preferred_element_type=f32)
            )
        for target, product in zip(targets, products):
            acc[target] += product
        return carry

    lax.fori_loop(0, (n + GROUP - 1) // GROUP, group, 0)


def forward_kernel(n_chunks, ids, places, count, tiles, *refs):
    chunks = refs[:n_chunks]
    own, other, gram_own, gram_other, acc, panel, tiles_here, gram, sems = refs[n_chunks:]
    z, x, y, core = ids[0], ids[1], ids[2], ids[3]
    pairs, at = [(tiles, tiles_here)], 0
    for chunk in chunks:
        pairs.append((chunk, panel.at[pl.ds(at, chunk.shape[0])]))
        at += chunk.shape[0]
    copies = start_copies(pairs, sems)
    acc[...] = jnp.zeros_like(acc)
    for copy in copies:
        copy.wait()

    def slot_index(p0, p1):
        c = p0 // 4
        return ((c & 1) ^ core) * 16 + ((c // 2 - y) & (NY - 1)) * 4 + (p0 & 3)

    def panel_tile(p0, p1):
        r = p1 // 2
        dz = (r // NX - z) & (NZ - 1)
        dx = (r - x) & (NX - 1)
        return (p1 & 1) * (NX * NZ) + dz * NX + dx

    tile_sums(count, places, tiles_here, panel, acc, slot_index, panel_tile, (((1,), (0,)), ((), ())))
    for d in range(NY):
        write_noted(own.at[d], acc, 4 * d, 4)
        write_noted(other.at[d], acc, 16 + 4 * d, 4)
    gram_into(gram, panel)
    half = RANK // 2
    gram_own[...] = gram[pl.ds(pl.multiple_of(core * half, half), half), :]
    gram_other[...] = gram[pl.ds(pl.multiple_of((1 - core) * half, half), half), :]


def forward(ids, places, count, tiles, chunks):
    slots = tiles.shape[0]
    return pl.pallas_call(
        functools.partial(forward_kernel, len(chunks)),
        out_shape=[
            jax.ShapeDtypeStruct((NY, 512 + NOTE, RANK), f32),
            jax.ShapeDtypeStruct((NY, 512 + NOTE, RANK), f32),
            jax.ShapeDtypeStruct((RANK // 2, RANK), f32),
            jax.ShapeDtypeStruct((RANK // 2, RANK), f32),
        ],
        in_specs=[IN_SMEM] * 3 + [ANYWHERE] * (1 + len(chunks)),
        out_specs=[IN_VMEM] * 4,
        scratch_shapes=[
            pltpu.VMEM((33, TILE, RANK), f32),
            pltpu.VMEM((8192, RANK), bf16),
            pltpu.VMEM((slots, TILE, TILE), bf16),
            pltpu.VMEM((RANK, RANK), f32),
            pltpu.SemaphoreType.DMA((1 + len(chunks),)),
        ],
        compiler_params=pltpu.CompilerParams(vmem_limit_bytes=VMEM_BYTES),
        name="forward",
    )(ids, places, count, tiles, *chunks)


def backward_kernel(ids, places, count, tiles, *refs):
    near, far = refs[:NY], refs[NY : 2 * NY]
    out_x, out_z, acc, panel, tiles_here, sems = refs[2 * NY :]
    z, x, y, core = ids[0], ids[1], ids[2], ids[3]
    pairs = [(tiles, tiles_here)]
    for d in range(NY):
        at = ((y + d) & (NY - 1)) * 2
        pairs.append((near[d], rows_at(panel, at + core, 512)))
        pairs.append((far[d], rows_at(panel, at + 1 - core, 512)))
    copies = start_copies(pairs, sems)
    acc[...] = jnp.zeros_like(acc)
    for copy in copies:
        copy.wait()

    def slot_index(p0, p1):
        r = p1 // 2
        dz = (r // NX - z) & (NZ - 1)
        dx = (r - x) & (NX - 1)
        return jnp.where((p1 & 1) == 0, dx * NZ + r // NX, NX * NZ + dz * NX + dx)

    tile_sums(count, places, tiles_here, panel, acc, slot_index, lambda p0, p1: p0, CONTRACT_0)
    for d in range(NX):
        for half in range(2):
            write_noted(out_x.at[d, half], acc, NZ * d + NZ // 2 * half, NZ // 2)
    for d in range(NZ):
        write_noted(out_z.at[d], acc, NX * NZ + NX * d, NX)


def backward(ids, places, count, tiles, near, far):
    slots = tiles.shape[0]
    return pl.pallas_call(
        backward_kernel,
        out_shape=[
            jax.ShapeDtypeStruct((NX, 2, NZ // 2 * TILE + NOTE, RANK), f32),
            jax.ShapeDtypeStruct((NZ, NX * TILE + NOTE, RANK), f32),
        ],
        in_specs=[IN_SMEM] * 3 + [ANYWHERE] * (1 + 2 * NY),
        out_specs=[IN_VMEM] * 2,
        scratch_shapes=[
            pltpu.VMEM((65, TILE, RANK), f32),
            pltpu.VMEM((4096, RANK), bf16),
            pltpu.VMEM((slots, TILE, TILE), bf16),
            pltpu.SemaphoreType.DMA((1 + 2 * NY,)),
        ],
        compiler_params=pltpu.CompilerParams(vmem_limit_bytes=VMEM_BYTES),
        name="backward",
    )(ids, places, count, tiles, *near, *far)


def hals_kernel(groups, gram_axis, n_gram, ids, x_ref, *refs):
    gram_refs, refs = refs[:n_gram], refs[n_gram:]
    n_parts = sum(count for _, count in groups)
    parts = refs[:n_parts]
    out_ref, xt, rt, gram = refs[n_parts:]
    n = x_ref.shape[0]
    size = RANK // len(gram_refs)
    for d, ref in enumerate(gram_refs):
        at = (ids[2] + d) & (NY - 1) if gram_axis == "y" else ids[3] ^ d
        gram[pl.ds(pl.multiple_of(at * size, size), size), :] = ref[...]
    g = gram[...]
    high = g.astype(bf16)
    rest = g - high.astype(f32)
    mid = rest.astype(bf16)
    low = (rest - mid.astype(f32)).astype(bf16)
    x = x_ref[...]
    xt[...] = x.astype(f32).T
    xg = lax.dot_general(low, x, CONTRACT_1, preferred_element_type=f32)
    xg = xg + lax.dot_general(mid, x, CONTRACT_1, preferred_element_type=f32)
    xg = xg + lax.dot_general(high, x, CONTRACT_1, preferred_element_type=f32)
    at = row = 0
    for rows, count in groups:
        target = add(*[part[...] for part in parts[at : at + count]])
        rt[:, row : row + rows] = target.T - xg[:, row : row + rows]
        at, row = at + count, row + rows
    shape = (RANK, RANK)
    diagonal = lax.broadcasted_iota(jnp.int32, shape, 0) == lax.broadcasted_iota(jnp.int32, shape, 1)
    inverse = 1.0 / (jnp.sum(jnp.where(diagonal, g, 0.0), axis=1, keepdims=True) + EPS)
    sublane = lax.broadcasted_iota(jnp.int32, (8, n), 0)
    for first in range(0, RANK, BLOCK):
        last = first + BLOCK
        remain = [rt[first + 8 * s : first + 8 * s + 8, :] for s in range(BLOCK // 8)]
        square = gram[first:last, first:last]
        changes = []
        for s in range(BLOCK // 8):
            at = first + 8 * s
            old = xt[at : at + 8, :]
            scale = jnp.broadcast_to(inverse[at : at + 8, :], (8, n))
            change = jnp.zeros((8, n), f32)
            for i in range(8):
                moved = jnp.maximum(old + remain[s] * scale, 0.0) - old
                change = jnp.where(sublane == i, moved, change)
                step = jnp.broadcast_to(moved[i : i + 1, :], (8, n))
                for t in range(s, BLOCK // 8):
                    remain[t] = remain[t] - square[8 * t : 8 * t + 8, 8 * s + i : 8 * s + i + 1] * step
            changes.append(change)
            xt[at : at + 8, :] = old + change
        if last < RANK:
            change = jnp.concatenate(changes, 0)
            change_high = change.astype(bf16)
            change_low = (change - change_high.astype(f32)).astype(bf16)
            update = jnp.dot(mid[last:, first:last], change_high, preferred_element_type=f32)
            update = update + jnp.dot(high[last:, first:last], change_low, preferred_element_type=f32)
            update = update + jnp.dot(high[last:, first:last], change_high, preferred_element_type=f32)
            rt[last:, :] = rt[last:, :] - update
    out_ref[...] = xt[...].T.astype(bf16)


def hals(ids, x, gram, gram_axis, groups):
    parts = [part for _, terms in groups for part in terms]
    spec = [(rows, len(terms)) for rows, terms in groups]
    n = x.shape[0]
    return pl.pallas_call(
        functools.partial(hals_kernel, spec, gram_axis, len(gram)),
        out_shape=jax.ShapeDtypeStruct((n, RANK), bf16),
        in_specs=[IN_SMEM] + [IN_VMEM] * (1 + len(gram) + len(parts)),
        out_specs=IN_VMEM,
        scratch_shapes=[
            pltpu.VMEM((RANK, n), f32),
            pltpu.VMEM((RANK, n), f32),
            pltpu.VMEM((RANK, RANK), f32),
        ],
        compiler_params=pltpu.CompilerParams(vmem_limit_bytes=VMEM_BYTES),
        name="hals",
    )(ids, x, *gram, *parts)


def gather_terms(term_factor):
    chunks = []
    for half, way in ((term_factor[:TILE], 1), (term_factor[TILE:], -1)):
        chunks += gather_ring(jnp.concatenate(gather_direct(half, NX, from_x), 0), NZ, from_z, way)
    return chunks


def sum_term_target(out_x, out_z, gram_rows):
    def hop(m, v):
        return encode(v + decode_all(m), wider(note_of(v), note_of(m)))

    def fresh(v):
        return encode(v, note_of(v))

    x_up, x_down = from_x(fresh(out_x[2, 0]), -1), from_x(fresh(out_x[2, 1]), 1)
    z_up, z_down = from_z(fresh(out_z[3]), -1), from_z(fresh(out_z[4]), 1)
    gram_rows = gram_rows + swap_z(gram_rows, 1)

    x_up, x_down, z_up, z_down = after((x_up, x_down, z_up, z_down), ())
    gram_rows = after(gram_rows, (z_up, z_down))
    x_up = from_x(jnp.stack([hop(x_up, out_x[1, 0]), fresh(out_x[1, 1])]), -1)
    x_down = from_x(jnp.stack([fresh(out_x[3, 0]), hop(x_down, out_x[3, 1])]), 1)
    z_up, z_down = from_z(hop(z_up, out_z[2]), -1), from_z(hop(z_down, out_z[5]), 1)
    gram_rows = gram_rows + swap_z(gram_rows, 2)

    z_up, z_down = after((z_up, z_down), ())
    gram_rows = after(gram_rows, (z_up, z_down))
    z_up, z_down = from_z(hop(z_up, out_z[1]), -1), from_z(hop(z_down, out_z[6]), 1)
    gram_rows = gram_rows + swap_z(gram_rows, 4)

    z_up, z_down = after((z_up, z_down), ())
    last = hop(z_down, out_z[7])
    x_up, x_down, gram_rows = after((x_up, x_down, gram_rows), last)
    z_down = from_z(last, 1)
    halves = []
    for half in range(2):
        total = out_x[0, half][:-NOTE] + decode(x_up[half]) + decode(x_down[half])
        note = wider(note_of(out_x[0, half]), note_of(x_up[half]), note_of(x_down[half]))
        halves.append(encode_each(total.reshape(NZ // 2, TILE, RANK), note))
    first = exchange_z(jnp.concatenate(halves, 0))
    gram = gather_direct(gram_rows, NY, from_y)

    total = out_z[0][:-NOTE] + decode(z_up) + decode(z_down)
    note = wider(note_of(out_z[0]), note_of(z_up), note_of(z_down))
    rows = encode_each(total.reshape(NX, TILE, RANK), note)
    second = total[:TILE]
    for d in range(1, NX):
        second = second + decode(from_x(rows[d], -d))
    return decode_sum(first), second, gram


def shards(tile_values, tile_places, tile_counts, doc_factor, term_factor):
    row, col = lax.axis_index("row"), lax.axis_index("col")
    ids = jnp.stack([row // NX, row % NX, col // 2, col % 2]).astype(jnp.int32)

    with jax.named_scope("gather_terms"):
        chunks = gather_terms(term_factor)
    own, other, gram_near, gram_far = forward(ids, tile_places, tile_counts, tile_values, chunks)

    with jax.named_scope("sum_doc_target"):
        arrived, gram_arrived = from_core(other), from_core(gram_far)
        target = (own[0] + arrived[0])[:-NOTE]
        messages = []
        for d in range(1, NY):
            messages.append(encode(own[d] + arrived[d], wider(note_of(own[d]), note_of(arrived[d]))))
        messages, gram_near = after((messages, gram_near + gram_arrived), ())
        landed = [from_y(m, -d) for d, m in enumerate(messages, 1)]
        gram_near = double(gram_near, swap_y, NY)
        gram_far = from_core(gram_near)
        landed = after(landed, gram_far)
        for m in landed:
            target = target + decode(m)

    new_doc = hals(ids, doc_factor, [gram_near, gram_far], "core", [(512, [target])])

    with jax.named_scope("gather_docs"):
        near = gather_direct(new_doc, NY, from_y)
        far = [from_core(chunk) for chunk in near]
    with jax.named_scope("doc_gram"):
        gram = sum(lax.dot_general(c, c, CONTRACT_0, preferred_element_type=f32) for c in near + far)
        gram_rows = lax.dynamic_slice_in_dim(gram, col // 2 * 64, 64, 0)
        gram_rows = add(*gather_direct(gram_rows, NX, from_x))
    out_x, out_z = backward(ids, tile_places, tile_counts, tile_values, near, far)

    with jax.named_scope("sum_term_target"):
        first, second, gram = sum_term_target(out_x, out_z, gram_rows)

    new_term = hals(ids, term_factor, gram, "y", [(TILE, [first]), (TILE, [second])])
    return new_doc, new_term


def solution(mesh):
    in_specs = (
        P(("row", "col"), None, None),
        P(("row", "col"), None),
        P(("row", "col")),
        P(("row", "col"), None),
        P(("col", "row"), None),
    )
    out_specs = (P(("row", "col"), None), P(("col", "row"), None))
    return jax.shard_map(shards, mesh=mesh, in_specs=in_specs, out_specs=out_specs, check_vma=False)
```

```python
import functools

import jax
import jax.numpy as jnp
from jax import lax
from jax.experimental import pallas as pl
from jax.experimental.pallas import tpu as pltpu
from jax.sharding import PartitionSpec as P

bf16, f16, f32 = jnp.bfloat16, jnp.float16, jnp.float32
NX, NZ, NY = 4, 8, 4
TILE, RANK = 128, 256
GROUP = 16
BLOCK = 64
EPS = 1e-06
NOTE = 16
VMEM_BYTES = 48 << 20

IN_VMEM = pl.BlockSpec(memory_space=pltpu.VMEM)
IN_SMEM = pl.BlockSpec(memory_space=pltpu.SMEM)
ANYWHERE = pl.BlockSpec(memory_space=pl.ANY)
CONTRACT_0 = (((0,), (0,)), ((), ()))
CONTRACT_1 = (((1,), (1,)), ((), ()))


def from_x(a, d):
    pairs = [(z * NX + (x + d) % NX, z * NX + x) for z in range(NZ) for x in range(NX)]
    return lax.ppermute(a, "row", pairs)


def from_z(a, d):
    pairs = [((z + d) % NZ * NX + x, z * NX + x) for z in range(NZ) for x in range(NX)]
    return lax.ppermute(a, "row", pairs)


def from_y(a, d):
    pairs = [((y + d) % NY * 2 + c, y * 2 + c) for y in range(NY) for c in range(2)]
    return lax.ppermute(a, "col", pairs)


def from_core(a):
    return lax.ppermute(a, "col", [(y * 2 + 1 - c, y * 2 + c) for y in range(NY) for c in range(2)])


def swap_z(a, hop):
    return lax.ppermute(a, "row", [(r ^ (hop * NX), r) for r in range(NZ * NX)])


def swap_y(a, hop):
    return lax.ppermute(a, "col", [(c ^ (hop * 2), c) for c in range(2 * NY)])


def after(values, deps):
    return lax.optimization_barrier((values, deps))[0]


def add(first, *rest):
    total = first.astype(f32)
    for term in rest:
        total = total + term.astype(f32)
    return total


def gather_direct(a, n, step):
    return [a] + [step(a, d) for d in range(1, n)]


def gather_ring(a, n, step, way):
    out = [None] * n
    out[0] = up = down = a
    for d in range(1, n // 2):
        up, down = step(up, 1), step(down, -1)
        out[d], out[n - d] = up, down
    out[n // 2] = step(up, 1) if way > 0 else step(down, -1)
    return out


def note_of(v):
    note = v[-NOTE:].astype(f32)
    return note[:1], note[NOTE // 2 : NOTE // 2 + 1] * 0.5


def wider(*notes):
    big, small = notes[0]
    for s, t in notes[1:]:
        big, small = jnp.maximum(big, s), jnp.minimum(small, t)
    return big, small


def encode(v, note):
    s, t = note
    row = lax.broadcasted_iota(jnp.int32, v.shape, 0) - (v.shape[0] - NOTE)
    return jnp.where(row < 0, v * t * t * t * t, jnp.where(row < NOTE // 2, s, t * 2.0)).astype(f16)


def encode_each(v, note):
    s, t = note
    lines = [jnp.broadcast_to(line, (v.shape[0], NOTE // 2, RANK)) for line in (s, t * 2.0)]
    return jnp.concatenate([v * t * t * t * t] + lines, 1).astype(f16)


def decode_all(m):
    s, _ = note_of(m)
    return m.astype(f32) * s * s * s * s


def decode(m):
    return decode_all(m)[:-NOTE]


def decode_sum(m):
    s = m[:, -NOTE : 1 - NOTE].astype(f32)
    return jnp.sum(m[:, :-NOTE].astype(f32) * s * s * s * s, 0)


def exchange_z(a):
    groups = [[z * NX + x for z in range(NZ)] for x in range(NX)]
    return lax.all_to_all(a, "row", 0, 0, axis_index_groups=groups)


def double(a, step, n):
    hop = 1
    while hop < n:
        a = a + step(a, hop)
        hop *= 2
    return a


def start_copies(pairs, sems):
    copies = [pltpu.make_async_copy(src, dst, sems.at[i]) for i, (src, dst) in enumerate(pairs)]
    for copy in copies:
        copy.start()
    return copies


def rows_at(ref, index, size):
    return ref.at[pl.ds(pl.multiple_of(index * size, size), size)]


def gram_into(ref, panel):
    rows = panel.shape[0]
    total = jnp.zeros((RANK, RANK), f32)
    for at in range(0, rows, 1024):
        part = panel[at : at + 1024, :]
        total = total + lax.dot_general(part, part, CONTRACT_0, preferred_element_type=f32)
    ref[...] = total


def write_noted(out, acc, first, count):
    tiles = acc[first : first + count]
    rows = count * TILE
    out[0:rows, :] = tiles.reshape(rows, RANK)
    top = jnp.max(jnp.max(tiles.reshape(rows // 8, 8, RANK), axis=0), axis=0, keepdims=True)
    e = jnp.ceil(jnp.log(jnp.maximum(top, 1e-30)) * 1.4426950408889634) - 11.0
    k = jnp.clip(jnp.ceil(e * 0.25), -14.0, 15.0)
    out[rows : rows + 8, :] = jnp.broadcast_to(jnp.exp2(k), (8, RANK))
    out[rows + 8 : rows + 16, :] = jnp.broadcast_to(jnp.exp2(1.0 - k), (8, RANK))


def tile_sums(count, places, tiles, panel, acc, slot_index, panel_tile, dims):
    n = count[0]
    spare = acc.shape[0] - 1

    def group(i, carry):
        targets, products = [], []
        for q in range(GROUP):
            s = i * GROUP + q
            p0, p1 = places[s, 0], places[s, 1]
            targets.append(jnp.where(s < n, slot_index(p0, p1), spare))
            at = pl.multiple_of(panel_tile(p0, p1) * TILE, TILE)
            products.append(
                lax.dot_general(tiles[s], panel[pl.ds(at, TILE), :], dims, preferred_element_type=f32)
            )
        for target, product in zip(targets, products):
            acc[target] += product
        return carry

    lax.fori_loop(0, (n + GROUP - 1) // GROUP, group, 0)


def forward_kernel(n_chunks, ids, places, count, tiles, *refs):
    chunks = refs[:n_chunks]
    own, other, gram_own, gram_other, acc, panel, tiles_here, gram, sems = refs[n_chunks:]
    z, x, y, core = ids[0], ids[1], ids[2], ids[3]
    pairs, at = [(tiles, tiles_here)], 0
    for chunk in chunks:
        pairs.append((chunk, panel.at[pl.ds(at, chunk.shape[0])]))
        at += chunk.shape[0]
    copies = start_copies(pairs, sems)
    acc[...] = jnp.zeros_like(acc)
    for copy in copies:
        copy.wait()

    def slot_index(p0, p1):
        c = p0 >> 2
        return ((c & 1) ^ core) * 16 + (((c >> 1) - y) & (NY - 1)) * 4 + (p0 & 3)

    def panel_tile(p0, p1):
        r = p1 >> 1
        dz = ((r >> 2) - z) & (NZ - 1)
        dx = (r - x) & (NX - 1)
        return (p1 & 1) * (NX * NZ) + dz * NX + dx

    tile_sums(count, places, tiles_here, panel, acc, slot_index, panel_tile, (((1,), (0,)), ((), ())))
    for d in range(NY):
        write_noted(own.at[d], acc, 4 * d, 4)
        write_noted(other.at[d], acc, 16 + 4 * d, 4)
    gram_into(gram, panel)
    half = RANK // 2
    gram_own[...] = gram[pl.ds(pl.multiple_of(core * half, half), half), :]
    gram_other[...] = gram[pl.ds(pl.multiple_of((1 - core) * half, half), half), :]


def forward(ids, places, count, tiles, chunks):
    slots = tiles.shape[0]
    return pl.pallas_call(
        functools.partial(forward_kernel, len(chunks)),
        out_shape=[
            jax.ShapeDtypeStruct((NY, 512 + NOTE, RANK), f32),
            jax.ShapeDtypeStruct((NY, 512 + NOTE, RANK), f32),
            jax.ShapeDtypeStruct((RANK // 2, RANK), f32),
            jax.ShapeDtypeStruct((RANK // 2, RANK), f32),
        ],
        in_specs=[IN_SMEM] * 3 + [ANYWHERE] * (1 + len(chunks)),
        out_specs=[IN_VMEM] * 4,
        scratch_shapes=[
            pltpu.VMEM((33, TILE, RANK), f32),
            pltpu.VMEM((8192, RANK), bf16),
            pltpu.VMEM((slots, TILE, TILE), bf16),
            pltpu.VMEM((RANK, RANK), f32),
            pltpu.SemaphoreType.DMA((1 + len(chunks),)),
        ],
        compiler_params=pltpu.CompilerParams(vmem_limit_bytes=VMEM_BYTES),
        name="forward",
    )(ids, places, count, tiles, *chunks)


def backward_kernel(ids, places, count, tiles, *refs):
    near, far = refs[:NY], refs[NY : 2 * NY]
    out_x, out_z, acc, panel, tiles_here, sems = refs[2 * NY :]
    z, x, y, core = ids[0], ids[1], ids[2], ids[3]
    pairs = [(tiles, tiles_here)]
    for d in range(NY):
        at = ((y + d) & (NY - 1)) * 2
        pairs.append((near[d], rows_at(panel, at + core, 512)))
        pairs.append((far[d], rows_at(panel, at + 1 - core, 512)))
    copies = start_copies(pairs, sems)
    acc[...] = jnp.zeros_like(acc)
    for copy in copies:
        copy.wait()

    def slot_index(p0, p1):
        r = p1 >> 1
        dz = ((r >> 2) - z) & (NZ - 1)
        dx = (r - x) & (NX - 1)
        return jnp.where((p1 & 1) == 0, dx * NZ + r // NX, NX * NZ + dz * NX + dx)

    tile_sums(count, places, tiles_here, panel, acc, slot_index, lambda p0, p1: p0, CONTRACT_0)
    for d in range(NX):
        for half in range(2):
            write_noted(out_x.at[d, half], acc, NZ * d + NZ // 2 * half, NZ // 2)
    for d in range(NZ):
        write_noted(out_z.at[d], acc, NX * NZ + NX * d, NX)


def backward(ids, places, count, tiles, near, far):
    slots = tiles.shape[0]
    return pl.pallas_call(
        backward_kernel,
        out_shape=[
            jax.ShapeDtypeStruct((NX, 2, NZ // 2 * TILE + NOTE, RANK), f32),
            jax.ShapeDtypeStruct((NZ, NX * TILE + NOTE, RANK), f32),
        ],
        in_specs=[IN_SMEM] * 3 + [ANYWHERE] * (1 + 2 * NY),
        out_specs=[IN_VMEM] * 2,
        scratch_shapes=[
            pltpu.VMEM((65, TILE, RANK), f32),
            pltpu.VMEM((4096, RANK), bf16),
            pltpu.VMEM((slots, TILE, TILE), bf16),
            pltpu.SemaphoreType.DMA((1 + 2 * NY,)),
        ],
        compiler_params=pltpu.CompilerParams(vmem_limit_bytes=VMEM_BYTES),
        name="backward",
    )(ids, places, count, tiles, *near, *far)


def hals_kernel(groups, gram_axis, n_gram, ids, x_ref, *refs):
    gram_refs, refs = refs[:n_gram], refs[n_gram:]
    n_parts = sum(count for _, count in groups)
    parts = refs[:n_parts]
    out_ref, xt, rt, gram = refs[n_parts:]
    n = x_ref.shape[0]
    size = RANK // len(gram_refs)
    for d, ref in enumerate(gram_refs):
        at = (ids[2] + d) & (NY - 1) if gram_axis == "y" else ids[3] ^ d
        gram[pl.ds(pl.multiple_of(at * size, size), size), :] = ref[...]
    g = gram[...]
    high = g.astype(bf16)
    rest = g - high.astype(f32)
    mid = rest.astype(bf16)
    low = (rest - mid.astype(f32)).astype(bf16)
    x = x_ref[...]
    xt[...] = x.astype(f32).T
    xg = lax.dot_general(low, x, CONTRACT_1, preferred_element_type=f32)
    xg = xg + lax.dot_general(mid, x, CONTRACT_1, preferred_element_type=f32)
    xg = xg + lax.dot_general(high, x, CONTRACT_1, preferred_element_type=f32)
    at = row = 0
    for rows, count in groups:
        target = add(*[part[0:rows, :] for part in parts[at : at + count]])
        rt[:, row : row + rows] = target.T - xg[:, row : row + rows]
        at, row = at + count, row + rows
    shape = (RANK, RANK)
    diagonal = lax.broadcasted_iota(jnp.int32, shape, 0) == lax.broadcasted_iota(jnp.int32, shape, 1)
    inverse = 1.0 / (jnp.sum(jnp.where(diagonal, g, 0.0), axis=1, keepdims=True) + EPS)
    sublane = lax.broadcasted_iota(jnp.int32, (8, n), 0)
    for first in range(0, RANK, BLOCK):
        last = first + BLOCK
        remain = [rt[first + 8 * s : first + 8 * s + 8, :] for s in range(BLOCK // 8)]
        square = gram[first:last, first:last]
        changes = []
        for s in range(BLOCK // 8):
            at = first + 8 * s
            old = xt[at : at + 8, :]
            scale = jnp.broadcast_to(inverse[at : at + 8, :], (8, n))
            change = jnp.zeros((8, n), f32)
            for i in range(8):
                moved = jnp.maximum(old + remain[s] * scale, 0.0) - old
                change = jnp.where(sublane == i, moved, change)
                step = jnp.broadcast_to(moved[i : i + 1, :], (8, n))
                for t in range(s, BLOCK // 8):
                    remain[t] = remain[t] - square[8 * t : 8 * t + 8, 8 * s + i : 8 * s + i + 1] * step
            changes.append(change)
            xt[at : at + 8, :] = old + change
        if last < RANK:
            change = jnp.concatenate(changes, 0)
            change_high = change.astype(bf16)
            change_low = (change - change_high.astype(f32)).astype(bf16)
            update = jnp.dot(mid[last:, first:last], change_high, preferred_element_type=f32)
            update = update + jnp.dot(high[last:, first:last], change_low, preferred_element_type=f32)
            update = update + jnp.dot(high[last:, first:last], change_high, preferred_element_type=f32)
            rt[last:, :] = rt[last:, :] - update
    out_ref[...] = xt[...].T.astype(bf16)


def hals(ids, x, gram, gram_axis, groups):
    parts = [part for _, terms in groups for part in terms]
    spec = [(rows, len(terms)) for rows, terms in groups]
    n = x.shape[0]
    return pl.pallas_call(
        functools.partial(hals_kernel, spec, gram_axis, len(gram)),
        out_shape=jax.ShapeDtypeStruct((n, RANK), bf16),
        in_specs=[IN_SMEM] + [IN_VMEM] * (1 + len(gram) + len(parts)),
        out_specs=IN_VMEM,
        scratch_shapes=[
            pltpu.VMEM((RANK, n), f32),
            pltpu.VMEM((RANK, n), f32),
            pltpu.VMEM((RANK, RANK), f32),
        ],
        compiler_params=pltpu.CompilerParams(vmem_limit_bytes=VMEM_BYTES),
        name="hals",
    )(ids, x, *gram, *parts)


def gather_terms(term_factor):
    chunks = []
    for half, way in ((term_factor[:TILE], 1), (term_factor[TILE:], -1)):
        chunks += gather_ring(jnp.concatenate(gather_direct(half, NX, from_x), 0), NZ, from_z, way)
    return chunks


def sum_term_target(out_x, out_z, gram_rows):
    def hop(m, v):
        return encode(v + decode_all(m), wider(note_of(v), note_of(m)))

    def fresh(v):
        return encode(v, note_of(v))

    x_up, x_down = from_x(fresh(out_x[2, 0]), -1), from_x(fresh(out_x[2, 1]), 1)
    z_up, z_down = from_z(fresh(out_z[3]), -1), from_z(fresh(out_z[4]), 1)
    gram_rows = gram_rows + swap_z(gram_rows, 4)

    x_up, x_down, z_up, z_down = after((x_up, x_down, z_up, z_down), ())
    gram_rows = after(gram_rows, (z_up, z_down))
    x_up = from_x(jnp.stack([hop(x_up, out_x[1, 0]), fresh(out_x[1, 1])]), -1)
    x_down = from_x(jnp.stack([fresh(out_x[3, 0]), hop(x_down, out_x[3, 1])]), 1)
    z_up, z_down = from_z(hop(z_up, out_z[2]), -1), from_z(hop(z_down, out_z[5]), 1)
    gram_rows = gram_rows + swap_z(gram_rows, 2)

    z_up, z_down = after((z_up, z_down), ())
    gram_rows = after(gram_rows, (z_up, z_down))
    z_up, z_down = from_z(hop(z_up, out_z[1]), -1), from_z(hop(z_down, out_z[6]), 1)
    gram_rows = gram_rows + swap_z(gram_rows, 1)

    z_up, z_down = after((z_up, z_down), ())
    last = hop(z_down, out_z[7])
    x_up, x_down, gram_rows = after((x_up, x_down, gram_rows), last)
    z_down = from_z(last, 1)
    halves = []
    for half in range(2):
        total = out_x[0, half][:-NOTE] + decode(x_up[half]) + decode(x_down[half])
        note = wider(note_of(out_x[0, half]), note_of(x_up[half]), note_of(x_down[half]))
        halves.append(encode_each(total.reshape(NZ // 2, TILE, RANK), note))
    first = exchange_z(jnp.concatenate(halves, 0))
    gram = gather_direct(gram_rows, NY, from_y)

    total = out_z[0][:-NOTE] + decode(z_up) + decode(z_down)
    note = wider(note_of(out_z[0]), note_of(z_up), note_of(z_down))
    rows = encode_each(total.reshape(NX, TILE, RANK), note)
    second = total[:TILE]
    for d in range(1, NX):
        second = second + decode(from_x(rows[d], -d))
    return decode_sum(first), second, gram


def shards(tile_values, tile_places, tile_counts, doc_factor, term_factor):
    row, col = lax.axis_index("row"), lax.axis_index("col")
    ids = jnp.stack([row // NX, row % NX, col // 2, col % 2]).astype(jnp.int32)

    with jax.named_scope("gather_terms"):
        chunks = gather_terms(term_factor)
    own, other, gram_near, gram_far = forward(ids, tile_places, tile_counts, tile_values, chunks)

    with jax.named_scope("sum_doc_target"):
        arrived, gram_arrived = from_core(other), from_core(gram_far)
        target = own[0] + arrived[0]
        messages = []
        for d in range(1, NY):
            messages.append(encode(own[d] + arrived[d], wider(note_of(own[d]), note_of(arrived[d]))))
        messages, gram_near = after((messages, gram_near + gram_arrived), ())
        landed = [from_y(m, -d) for d, m in enumerate(messages, 1)]
        gram_near = double(gram_near, swap_y, NY)
        gram_far = from_core(gram_near)
        landed = after(landed, gram_far)
        for m in landed:
            target = target + decode_all(m)

    new_doc = hals(ids, doc_factor, [gram_near, gram_far], "core", [(512, [target])])

    with jax.named_scope("gather_docs"):
        near = gather_direct(new_doc, NY, from_y)
        far = [from_core(chunk) for chunk in near]
    with jax.named_scope("doc_gram"):
        gram = sum(lax.dot_general(c, c, CONTRACT_0, preferred_element_type=f32) for c in near + far)
        gram_rows = lax.dynamic_slice_in_dim(gram, col // 2 * 64, 64, 0)
        gram_rows = add(*gather_direct(gram_rows, NX, from_x))
    out_x, out_z = backward(ids, tile_places, tile_counts, tile_values, near, far)

    with jax.named_scope("sum_term_target"):
        first, second, gram = sum_term_target(out_x, out_z, gram_rows)

    new_term = hals(ids, term_factor, gram, "y", [(TILE, [first]), (TILE, [second])])
    return new_doc, new_term


def solution(mesh):
    in_specs = (
        P(("row", "col"), None, None),
        P(("row", "col"), None),
        P(("row", "col")),
        P(("row", "col"), None),
        P(("col", "row"), None),
    )
    out_specs = (P(("row", "col"), None), P(("col", "row"), None))
    return jax.shard_map(shards, mesh=mesh, in_specs=in_specs, out_specs=out_specs, check_vma=False)
```

```python
import functools

import jax
import jax.numpy as jnp
from jax import lax
from jax.experimental import pallas as pl
from jax.experimental.pallas import tpu as pltpu
from jax.sharding import PartitionSpec as P

bf16, f16, f32 = jnp.bfloat16, jnp.float16, jnp.float32
NX, NZ, NY = 4, 8, 4
TILE, RANK = 128, 256
GROUP = 16
BLOCK = 64
EPS = 1e-06
NOTE = 16
VMEM_BYTES = 48 << 20

IN_VMEM = pl.BlockSpec(memory_space=pltpu.VMEM)
IN_SMEM = pl.BlockSpec(memory_space=pltpu.SMEM)
ANYWHERE = pl.BlockSpec(memory_space=pl.ANY)
CONTRACT_0 = (((0,), (0,)), ((), ()))
CONTRACT_1 = (((1,), (1,)), ((), ()))


def from_x(a, d):
    pairs = [(z * NX + (x + d) % NX, z * NX + x) for z in range(NZ) for x in range(NX)]
    return lax.ppermute(a, "row", pairs)


def from_z(a, d):
    pairs = [((z + d) % NZ * NX + x, z * NX + x) for z in range(NZ) for x in range(NX)]
    return lax.ppermute(a, "row", pairs)


def from_y(a, d):
    pairs = [((y + d) % NY * 2 + c, y * 2 + c) for y in range(NY) for c in range(2)]
    return lax.ppermute(a, "col", pairs)


def from_core(a):
    return lax.ppermute(a, "col", [(y * 2 + 1 - c, y * 2 + c) for y in range(NY) for c in range(2)])


def swap_z(a, hop):
    return lax.ppermute(a, "row", [(r ^ (hop * NX), r) for r in range(NZ * NX)])


def swap_y(a, hop):
    return lax.ppermute(a, "col", [(c ^ (hop * 2), c) for c in range(2 * NY)])


def after(values, deps):
    return lax.optimization_barrier((values, deps))[0]


def add(first, *rest):
    total = first.astype(f32)
    for term in rest:
        total = total + term.astype(f32)
    return total


def gather_direct(a, n, step):
    return [a] + [step(a, d) for d in range(1, n)]


def gather_ring(a, n, step, way):
    out = [None] * n
    out[0] = up = down = a
    for d in range(1, n // 2):
        up, down = step(up, 1), step(down, -1)
        out[d], out[n - d] = up, down
    out[n // 2] = step(up, 1) if way > 0 else step(down, -1)
    return out


def note_of(v):
    note = v[-NOTE:].astype(f32)
    return note[:1], note[NOTE // 2 : NOTE // 2 + 1] * 0.5


def wider(*notes):
    big, small = notes[0]
    for s, t in notes[1:]:
        big, small = jnp.maximum(big, s), jnp.minimum(small, t)
    return big, small


def encode(v, note):
    s, t = note
    row = lax.broadcasted_iota(jnp.int32, v.shape, 0) - (v.shape[0] - NOTE)
    return jnp.where(row < 0, v * t * t * t * t, jnp.where(row < NOTE // 2, s, t * 2.0)).astype(f16)


def encode_each(v, note):
    s, t = note
    lines = [jnp.broadcast_to(line, (v.shape[0], NOTE // 2, RANK)) for line in (s, t * 2.0)]
    return jnp.concatenate([v * t * t * t * t] + lines, 1).astype(f16)


def decode_all(m):
    s, _ = note_of(m)
    return m.astype(f32) * s * s * s * s


def decode(m):
    return decode_all(m)[:-NOTE]


def decode_sum(m):
    s = m[:, -NOTE : 1 - NOTE].astype(f32)
    return jnp.sum(m[:, :-NOTE].astype(f32) * s * s * s * s, 0)


def exchange_z(a):
    groups = [[z * NX + x for z in range(NZ)] for x in range(NX)]
    return lax.all_to_all(a, "row", 0, 0, axis_index_groups=groups)


def double(a, step, n):
    hop = 1
    while hop < n:
        a = a + step(a, hop)
        hop *= 2
    return a


def start_copies(pairs, sems):
    copies = [pltpu.make_async_copy(src, dst, sems.at[i]) for i, (src, dst) in enumerate(pairs)]
    for copy in copies:
        copy.start()
    return copies


def rows_at(ref, index, size):
    return ref.at[pl.ds(pl.multiple_of(index * size, size), size)]


def gram_into(ref, panel):
    rows = panel.shape[0]
    total = jnp.zeros((RANK, RANK), f32)
    for at in range(0, rows, 1024):
        part = panel[at : at + 1024, :]
        total = total + lax.dot_general(part, part, CONTRACT_0, preferred_element_type=f32)
    ref[...] = total


def write_noted(out, acc, first, count, scaled=False):
    tiles = acc[first : first + count]
    rows = count * TILE
    top = jnp.max(jnp.max(tiles.reshape(rows // 8, 8, RANK), axis=0), axis=0, keepdims=True)
    e = jnp.ceil(jnp.log(jnp.maximum(top, 1e-30)) * 1.4426950408889634) - 11.0
    k = jnp.clip(jnp.ceil(e * 0.25), -14.0, 15.0)
    values = tiles.reshape(rows, RANK)
    if scaled:
        t = jnp.exp2(-k)
        values = values * t * t * t * t
    out[0:rows, :] = values
    out[rows : rows + 8, :] = jnp.broadcast_to(jnp.exp2(k), (8, RANK))
    out[rows + 8 : rows + 16, :] = jnp.broadcast_to(jnp.exp2(1.0 - k), (8, RANK))


def tile_sums(count, places, tiles, panel, acc, slot_index, panel_tile, dims):
    n = count[0]
    spare = acc.shape[0] - 1

    def group(i, carry):
        targets, products = [], []
        for q in range(GROUP):
            s = i * GROUP + q
            p0, p1 = places[s, 0], places[s, 1]
            targets.append(jnp.where(s < n, slot_index(p0, p1), spare))
            at = pl.multiple_of(panel_tile(p0, p1) * TILE, TILE)
            products.append(
                lax.dot_general(tiles[s], panel[pl.ds(at, TILE), :], dims, preferred_element_type=f32)
            )
        for target, product in zip(targets, products):
            acc[target] += product
        return carry

    lax.fori_loop(0, (n + GROUP - 1) // GROUP, group, 0)


def forward_kernel(n_chunks, ids, places, count, tiles, *refs):
    chunks = refs[:n_chunks]
    own, other, gram_own, gram_other, acc, panel, tiles_here, gram, sems = refs[n_chunks:]
    z, x, y, core = ids[0], ids[1], ids[2], ids[3]
    pairs, at = [(tiles, tiles_here)], 0
    for chunk in chunks:
        pairs.append((chunk, panel.at[pl.ds(at, chunk.shape[0])]))
        at += chunk.shape[0]
    copies = start_copies(pairs, sems)
    acc[...] = jnp.zeros_like(acc)
    for copy in copies:
        copy.wait()

    def slot_index(p0, p1):
        c = p0 >> 2
        return ((c & 1) ^ core) * 16 + (((c >> 1) - y) & (NY - 1)) * 4 + (p0 & 3)

    def panel_tile(p0, p1):
        r = p1 >> 1
        dz = ((r >> 2) - z) & (NZ - 1)
        dx = (r - x) & (NX - 1)
        return (p1 & 1) * (NX * NZ) + dz * NX + dx

    tile_sums(count, places, tiles_here, panel, acc, slot_index, panel_tile, (((1,), (0,)), ((), ())))
    for d in range(NY):
        write_noted(own.at[d], acc, 4 * d, 4)
        write_noted(other.at[d], acc, 16 + 4 * d, 4)
    gram_into(gram, panel)
    half = RANK // 2
    gram_own[...] = gram[pl.ds(pl.multiple_of(core * half, half), half), :]
    gram_other[...] = gram[pl.ds(pl.multiple_of((1 - core) * half, half), half), :]


def forward(ids, places, count, tiles, chunks):
    slots = tiles.shape[0]
    return pl.pallas_call(
        functools.partial(forward_kernel, len(chunks)),
        out_shape=[
            jax.ShapeDtypeStruct((NY, 512 + NOTE, RANK), f32),
            jax.ShapeDtypeStruct((NY, 512 + NOTE, RANK), f32),
            jax.ShapeDtypeStruct((RANK // 2, RANK), f32),
            jax.ShapeDtypeStruct((RANK // 2, RANK), f32),
        ],
        in_specs=[IN_SMEM] * 3 + [ANYWHERE] * (1 + len(chunks)),
        out_specs=[IN_VMEM] * 4,
        scratch_shapes=[
            pltpu.VMEM((33, TILE, RANK), f32),
            pltpu.VMEM((8192, RANK), bf16),
            pltpu.VMEM((slots, TILE, TILE), bf16),
            pltpu.VMEM((RANK, RANK), f32),
            pltpu.SemaphoreType.DMA((1 + len(chunks),)),
        ],
        compiler_params=pltpu.CompilerParams(vmem_limit_bytes=VMEM_BYTES),
        name="forward",
    )(ids, places, count, tiles, *chunks)


def backward_kernel(ids, places, count, tiles, *refs):
    near, far = refs[:NY], refs[NY : 2 * NY]
    out_x, out_z, acc, panel, tiles_here, sems = refs[2 * NY :]
    z, x, y, core = ids[0], ids[1], ids[2], ids[3]
    pairs = [(tiles, tiles_here)]
    for d in range(NY):
        at = ((y + d) & (NY - 1)) * 2
        pairs.append((near[d], rows_at(panel, at + core, 512)))
        pairs.append((far[d], rows_at(panel, at + 1 - core, 512)))
    copies = start_copies(pairs, sems)
    acc[...] = jnp.zeros_like(acc)
    for copy in copies:
        copy.wait()

    def slot_index(p0, p1):
        r = p1 >> 1
        dz = ((r >> 2) - z) & (NZ - 1)
        dx = (r - x) & (NX - 1)
        return jnp.where((p1 & 1) == 0, dx * NZ + r // NX, NX * NZ + dz * NX + dx)

    tile_sums(count, places, tiles_here, panel, acc, slot_index, lambda p0, p1: p0, CONTRACT_0)
    for d in range(NX):
        for half in range(2):
            scaled = (d, half) in ((2, 0), (2, 1), (1, 1), (3, 0))
            write_noted(out_x.at[d, half], acc, NZ * d + NZ // 2 * half, NZ // 2, scaled)
    for d in range(NZ):
        write_noted(out_z.at[d], acc, NX * NZ + NX * d, NX, d in (3, 4))


def backward(ids, places, count, tiles, near, far):
    slots = tiles.shape[0]
    return pl.pallas_call(
        backward_kernel,
        out_shape=[
            jax.ShapeDtypeStruct((NX, 2, NZ // 2 * TILE + NOTE, RANK), f32),
            jax.ShapeDtypeStruct((NZ, NX * TILE + NOTE, RANK), f32),
        ],
        in_specs=[IN_SMEM] * 3 + [ANYWHERE] * (1 + 2 * NY),
        out_specs=[IN_VMEM] * 2,
        scratch_shapes=[
            pltpu.VMEM((65, TILE, RANK), f32),
            pltpu.VMEM((4096, RANK), bf16),
            pltpu.VMEM((slots, TILE, TILE), bf16),
            pltpu.SemaphoreType.DMA((1 + 2 * NY,)),
        ],
        compiler_params=pltpu.CompilerParams(vmem_limit_bytes=VMEM_BYTES),
        name="backward",
    )(ids, places, count, tiles, *near, *far)


def hals_kernel(groups, gram_axis, n_gram, ids, x_ref, *refs):
    gram_refs, refs = refs[:n_gram], refs[n_gram:]
    n_parts = sum(count for _, count in groups)
    parts = refs[:n_parts]
    out_ref, xt, rt, gram = refs[n_parts:]
    n = x_ref.shape[0]
    size = RANK // len(gram_refs)
    for d, ref in enumerate(gram_refs):
        at = (ids[2] + d) & (NY - 1) if gram_axis == "y" else ids[3] ^ d
        gram[pl.ds(pl.multiple_of(at * size, size), size), :] = ref[...]
    g = gram[...]
    high = g.astype(bf16)
    rest = g - high.astype(f32)
    mid = rest.astype(bf16)
    low = (rest - mid.astype(f32)).astype(bf16)
    x = x_ref[...]
    xt[...] = x.astype(f32).T
    xg = lax.dot_general(low, x, CONTRACT_1, preferred_element_type=f32)
    xg = xg + lax.dot_general(mid, x, CONTRACT_1, preferred_element_type=f32)
    xg = xg + lax.dot_general(high, x, CONTRACT_1, preferred_element_type=f32)
    at = row = 0
    for rows, count in groups:
        target = add(*[part[0:rows, :] for part in parts[at : at + count]])
        rt[:, row : row + rows] = target.T - xg[:, row : row + rows]
        at, row = at + count, row + rows
    shape = (RANK, RANK)
    diagonal = lax.broadcasted_iota(jnp.int32, shape, 0) == lax.broadcasted_iota(jnp.int32, shape, 1)
    inverse = 1.0 / (jnp.sum(jnp.where(diagonal, g, 0.0), axis=1, keepdims=True) + EPS)
    sublane = lax.broadcasted_iota(jnp.int32, (8, n), 0)
    for first in range(0, RANK, BLOCK):
        last = first + BLOCK
        remain = [rt[first + 8 * s : first + 8 * s + 8, :] for s in range(BLOCK // 8)]
        square = gram[first:last, first:last]
        changes = []
        for s in range(BLOCK // 8):
            at = first + 8 * s
            old = xt[at : at + 8, :]
            scale = jnp.broadcast_to(inverse[at : at + 8, :], (8, n))
            change = jnp.zeros((8, n), f32)
            for i in range(8):
                moved = jnp.maximum(old + remain[s] * scale, 0.0) - old
                change = jnp.where(sublane == i, moved, change)
                step = jnp.broadcast_to(moved[i : i + 1, :], (8, n))
                for t in range(s, BLOCK // 8):
                    remain[t] = remain[t] - square[8 * t : 8 * t + 8, 8 * s + i : 8 * s + i + 1] * step
            changes.append(change)
            xt[at : at + 8, :] = old + change
        if last < RANK:
            change = jnp.concatenate(changes, 0)
            change_high = change.astype(bf16)
            change_low = (change - change_high.astype(f32)).astype(bf16)
            update = jnp.dot(mid[last:, first:last], change_high, preferred_element_type=f32)
            update = update + jnp.dot(high[last:, first:last], change_low, preferred_element_type=f32)
            update = update + jnp.dot(high[last:, first:last], change_high, preferred_element_type=f32)
            rt[last:, :] = rt[last:, :] - update
    out_ref[...] = xt[...].T.astype(bf16)


def hals(ids, x, gram, gram_axis, groups):
    parts = [part for _, terms in groups for part in terms]
    spec = [(rows, len(terms)) for rows, terms in groups]
    n = x.shape[0]
    return pl.pallas_call(
        functools.partial(hals_kernel, spec, gram_axis, len(gram)),
        out_shape=jax.ShapeDtypeStruct((n, RANK), bf16),
        in_specs=[IN_SMEM] + [IN_VMEM] * (1 + len(gram) + len(parts)),
        out_specs=IN_VMEM,
        scratch_shapes=[
            pltpu.VMEM((RANK, n), f32),
            pltpu.VMEM((RANK, n), f32),
            pltpu.VMEM((RANK, RANK), f32),
        ],
        compiler_params=pltpu.CompilerParams(vmem_limit_bytes=VMEM_BYTES),
        name="hals",
    )(ids, x, *gram, *parts)


def gather_terms(term_factor):
    chunks = []
    for half, way in ((term_factor[:TILE], 1), (term_factor[TILE:], -1)):
        chunks += gather_ring(jnp.concatenate(gather_direct(half, NX, from_x), 0), NZ, from_z, way)
    return chunks


def sum_term_target(out_x, out_z, gram_rows):
    def hop(m, v):
        return encode(v + decode_all(m), wider(note_of(v), note_of(m)))

    def fresh(v):
        return v.astype(f16)

    x_up, x_down = from_x(fresh(out_x[2, 0]), -1), from_x(fresh(out_x[2, 1]), 1)
    z_up, z_down = from_z(fresh(out_z[3]), -1), from_z(fresh(out_z[4]), 1)
    gram_rows = gram_rows + swap_z(gram_rows, 4)

    x_up, x_down, z_up, z_down = after((x_up, x_down, z_up, z_down), ())
    gram_rows = after(gram_rows, (z_up, z_down))
    x_up = from_x(jnp.stack([hop(x_up, out_x[1, 0]), fresh(out_x[1, 1])]), -1)
    x_down = from_x(jnp.stack([fresh(out_x[3, 0]), hop(x_down, out_x[3, 1])]), 1)
    z_up, z_down = from_z(hop(z_up, out_z[2]), -1), from_z(hop(z_down, out_z[5]), 1)
    gram_rows = gram_rows + swap_z(gram_rows, 2)

    z_up, z_down = after((z_up, z_down), ())
    gram_rows = after(gram_rows, (z_up, z_down))
    z_up, z_down = from_z(hop(z_up, out_z[1]), -1), from_z(hop(z_down, out_z[6]), 1)
    gram_rows = gram_rows + swap_z(gram_rows, 1)

    z_up, z_down = after((z_up, z_down), ())
    last = hop(z_down, out_z[7])
    x_up, x_down, gram_rows = after((x_up, x_down, gram_rows), last)
    z_down = from_z(last, 1)
    halves = []
    for half in range(2):
        total = out_x[0, half][:-NOTE] + decode(x_up[half]) + decode(x_down[half])
        note = wider(note_of(out_x[0, half]), note_of(x_up[half]), note_of(x_down[half]))
        halves.append(encode_each(total.reshape(NZ // 2, TILE, RANK), note))
    first = exchange_z(jnp.concatenate(halves, 0))
    gram = gather_direct(gram_rows, NY, from_y)

    total = out_z[0][:-NOTE] + decode(z_up) + decode(z_down)
    note = wider(note_of(out_z[0]), note_of(z_up), note_of(z_down))
    rows = encode_each(total.reshape(NX, TILE, RANK), note)
    second = total[:TILE]
    for d in range(1, NX):
        second = second + decode(from_x(rows[d], -d))
    return decode_sum(first), second, gram


def shards(tile_values, tile_places, tile_counts, doc_factor, term_factor):
    row, col = lax.axis_index("row"), lax.axis_index("col")
    ids = jnp.stack([row // NX, row % NX, col // 2, col % 2]).astype(jnp.int32)

    with jax.named_scope("gather_terms"):
        chunks = gather_terms(term_factor)
    own, other, gram_near, gram_far = forward(ids, tile_places, tile_counts, tile_values, chunks)

    with jax.named_scope("sum_doc_target"):
        arrived, gram_arrived = from_core(other), from_core(gram_far)
        target = own[0] + arrived[0]
        messages = []
        for d in range(1, NY):
            messages.append(encode(own[d] + arrived[d], wider(note_of(own[d]), note_of(arrived[d]))))
        messages, gram_near = after((messages, gram_near + gram_arrived), ())
        landed = [from_y(m, -d) for d, m in enumerate(messages, 1)]
        gram_near = double(gram_near, swap_y, NY)
        gram_far = from_core(gram_near)
        landed = after(landed, gram_far)
        for m in landed:
            target = target + decode_all(m)

    new_doc = hals(ids, doc_factor, [gram_near, gram_far], "core", [(512, [target])])

    with jax.named_scope("gather_docs"):
        near = gather_direct(new_doc, NY, from_y)
        far = [from_core(chunk) for chunk in near]
    with jax.named_scope("doc_gram"):
        gram = sum(lax.dot_general(c, c, CONTRACT_0, preferred_element_type=f32) for c in near + far)
        gram_rows = lax.dynamic_slice_in_dim(gram, col // 2 * 64, 64, 0)
        gram_rows = add(*gather_direct(gram_rows, NX, from_x))
    out_x, out_z = backward(ids, tile_places, tile_counts, tile_values, near, far)

    with jax.named_scope("sum_term_target"):
        first, second, gram = sum_term_target(out_x, out_z, gram_rows)

    new_term = hals(ids, term_factor, gram, "y", [(TILE, [first]), (TILE, [second])])
    return new_doc, new_term


def solution(mesh):
    in_specs = (
        P(("row", "col"), None, None),
        P(("row", "col"), None),
        P(("row", "col")),
        P(("row", "col"), None),
        P(("col", "row"), None),
    )
    out_specs = (P(("row", "col"), None), P(("col", "row"), None))
    return jax.shard_map(shards, mesh=mesh, in_specs=in_specs, out_specs=out_specs, check_vma=False)
```
